32 devices in a mesh: dp: 16 (over z, y, core), tensor: 2 (over x).
Axes of the slice: x: 2, y: 2, z: 4, core: 2. Of those that a mesh axis runs over, the one named last changes fastest.
Arguments:
- inputs: float32 [4096, 1024], P('dp', 'tensor'), may hold values from -6 to 6
- cotangent: float32 [4096, 1024], P('dp', 'tensor'), may hold values from -0.12 to 0.12
- gate_weight: float32 [1024, 4096], P('dp', 'tensor'), may hold values from -0.1875 to 0.1875
- up_weight: float32 [1024, 4096], P('dp', 'tensor'), may hold values from -0.1875 to 0.1875
- down_weight: float32 [1024, 4096], P('dp', 'tensor'), may hold values from -0.09375 to 0.09375
- gate_first: float32 [1024, 4096], P('dp', 'tensor'), may hold values from -6 to 6
- gate_second: float32 [1024, 4096], P('dp', 'tensor'), may hold values from 0.5 to 4
- up_first: float32 [1024, 4096], P('dp', 'tensor'), may hold values from -6 to 6
- up_second: float32 [1024, 4096], P('dp', 'tensor'), may hold values from 0.5 to 4
Outputs:
- gate_new: float32 [1024, 4096], P('dp', 'tensor')
- gate_first_new: float32 [1024, 4096], P('dp', 'tensor')
- gate_second_new: float32 [1024, 4096], P('dp', 'tensor')
- up_new: float32 [1024, 4096], P('dp', 'tensor')
- up_first_new: float32 [1024, 4096], P('dp', 'tensor')
- up_second_new: float32 [1024, 4096], P('dp', 'tensor')
The draws below stay inside these ranges and needn't reach their ends.
All inputs are finite; a program needn't handle non-finite values.
Results may differ from the reference program's by a relative error of at most 0.00005.
Values sent between devices are 32-bit elements; how exact they have to be, the bound alone decides.
No kernel may reach another device: no remote copies, remote signals or barrier semaphores. Data moves between devices by JAX's collectives and lax.ppermute only.
A program may use at most 64 MiB of HBM per device.

```python
import math
import jax
import jax.numpy as jnp
from jax import lax

D = 1024
FF = 4096
STEP = 100
TOKENS = 4096
N_TENSOR = 2


def raised(entries, own_key, source, target, shards_of, factor):
    def block_of(axis_at):
        return (jnp.arange(entries.shape[axis_at]) // (entries.shape[axis_at] // shards_of)).reshape((-1,) + (1,) * (entries.ndim - 1 - axis_at))

    first = jax.random.permutation(own_key, shards_of)[block_of(target)]
    far = (block_of(target) + shards_of // 2) % shards_of
    return jnp.where((block_of(source) == first) | (block_of(source) == far), factor * entries, entries)


def block_levels(rng, shape, shards, low, top_value):
    factor_of, own = 1.0, jax.random.fold_in(rng, 6)
    for axis_at, blocks in shards:
        steps = jnp.exp(jax.random.uniform(jax.random.fold_in(own, axis_at), (blocks,), jnp.float32, low / len(shards), top_value / len(shards)))
        factor_of = factor_of * jnp.repeat(steps, shape[axis_at] // blocks).reshape([-1 if axis == axis_at else 1 for axis in range(len(shape))])
    return factor_of


def gaussian(own_key, shape, scale, bound, shards=(), dtype=jnp.bfloat16):
    level = block_levels(own_key, shape, shards, -0.22, 0.18) if shards else 1.0
    values = jax.random.normal(own_key, shape, jnp.float32) * scale * level
    return jnp.minimum(jnp.maximum(values, -bound), bound).astype(dtype)


def gaussian_with(rng, extent, scale, bound, cuts, heavy, held_as=jnp.bfloat16):
    array = scale * jax.random.normal(rng, extent, jnp.float32)
    if cuts:
        array = array * block_levels(rng, extent, cuts, -0.22, 0.18)
    return jnp.clip(raised(array, jax.random.fold_in(rng, 3), *heavy), -bound, bound).astype(held_as)


def setup_inputs(seed: int = 0) -> dict:
    keys = jax.random.split(jax.random.key(seed), 10)
    return {
        "inputs": gaussian_with(keys[0], (TOKENS, D), 1.0, 6.0, ((0, 16), (1, 2)), (0, 1, 16, 2.0), jnp.float32),
        "cotangent": gaussian(keys[1], (TOKENS, D), 0.02, 0.12, ((0, 16), (1, 2)), jnp.float32),
        "gate_weight": gaussian(keys[2], (D, FF), D ** -0.5, 0.1875, ((0, 16), (1, 2)), jnp.float32),
        "up_weight": gaussian(keys[3], (D, FF), D ** -0.5, 0.1875, ((0, 16), (1, 2)), jnp.float32),
        "down_weight": gaussian(keys[4], (D, FF), FF ** -0.5, 0.09375, ((0, 16), (1, 2)), jnp.float32),
        "gate_first": gaussian(keys[5], (D, FF), 1.0, 6.0, ((0, 16), (1, 2)), jnp.float32),
        "gate_second": jnp.clip(jnp.exp(math.log(4.0) - 2.0794415 * jax.random.uniform(keys[6], (D, FF), jnp.float32) ** block_levels(keys[6], (D, FF), ((0, 16), (1, 2)), -0.2, 0.2)), 0.5, 4.0),
        "up_first": gaussian(keys[7], (D, FF), 1.0, 6.0, ((0, 16), (1, 2)), jnp.float32),
        "up_second": jnp.clip(jnp.exp(math.log(4.0) - 2.0794415 * jax.random.uniform(keys[8], (D, FF), jnp.float32) ** block_levels(keys[8], (D, FF), ((0, 16), (1, 2)), -0.2, 0.2)), 0.5, 4.0),
    }


def adam_update(weight, first, second, grad):
    first_new = 0.9 * first + 0.1 * grad
    second_new = 0.95 * second + 0.05 * grad * grad
    first_hat = first_new / (1.0 - 0.9 ** STEP)
    second_hat = second_new / (1.0 - 0.95 ** STEP)
    weight_new = weight - 0.003 * first_hat / (jnp.sqrt(second_hat) + 1e-08)
    return (weight_new, first_new, second_new)

def reference(inputs, cotangent, gate_weight, up_weight, down_weight, gate_first, gate_second, up_first, up_second):
    highest = lax.Precision.HIGHEST
    block_count = N_TENSOR
    block_width = FF // block_count

    def split_cols(weight):
        return jnp.transpose(weight.reshape(D, block_count, block_width), (1, 0, 2))

    def one_block(blocks):
        gate_part, lift_part, down_part = blocks
        gate_sum = jnp.dot(inputs, gate_part, precision=highest, preferred_element_type=jnp.float32)
        lift_sum = jnp.dot(inputs, lift_part, precision=highest, preferred_element_type=jnp.float32)
        back_sum = jnp.dot(cotangent, down_part, precision=highest, preferred_element_type=jnp.float32)
        sigmoid_gate = jax.nn.sigmoid(gate_sum)
        gate_rows = back_sum * lift_sum * sigmoid_gate * (1.0 + gate_sum * (1.0 - sigmoid_gate))
        lift_rows = back_sum * gate_sum * sigmoid_gate
        dims = (((0,), (0,)), ((), ()))
        gate_grad = lax.dot_general(inputs, gate_rows, dims, precision=highest, preferred_element_type=jnp.float32)
        lift_grad = lax.dot_general(inputs, lift_rows, dims, precision=highest, preferred_element_type=jnp.float32)
        return (gate_grad, lift_grad)
    gate_blocks, lift_blocks = lax.map(one_block, (split_cols(gate_weight), split_cols(up_weight), split_cols(down_weight)))
    gate_grad = jnp.transpose(gate_blocks, (1, 0, 2)).reshape(D, FF)
    lift_grad = jnp.transpose(lift_blocks, (1, 0, 2)).reshape(D, FF)
    gate_new, gate_first_new, gate_second_new = adam_update(gate_weight, gate_first, gate_second, gate_grad)
    up_new, up_first_new, up_second_new = adam_update(up_weight, up_first, up_second, lift_grad)
    return (gate_new, gate_first_new, gate_second_new, up_new, up_first_new, up_second_new)
```

```python
import jax
import jax.numpy as jnp
from jax import lax
from jax.sharding import PartitionSpec as P

STEP = 100
CHUNKS = 4
PRECISION = lax.Precision.HIGH


def adam_update(weight, first, second, grad):
    first_new = 0.9 * first + 0.1 * grad
    second_new = 0.95 * second + 0.05 * grad * grad
    first_hat = first_new / (1.0 - 0.9**STEP)
    second_hat = second_new / (1.0 - 0.95**STEP)
    weight_new = weight - 0.003 * first_hat / (jnp.sqrt(second_hat) + 1e-08)
    return (weight_new, first_new, second_new)


def contract(left, right, left_dim):
    return lax.dot_general(
        left,
        right,
        (((left_dim,), (0,)), ((), ())),
        precision=PRECISION,
        preferred_element_type=jnp.float32,
    )


class Bit:
    def __init__(self, axis, size, place):
        self.axis = axis
        self.pairs = [(i, i ^ (1 << place)) for i in range(size)]
        self.mine = (lax.axis_index(axis) >> place) & 1

    def swap(self, array):
        return lax.ppermute(array, self.axis, self.pairs)

    def own(self, array, dim):
        return lax.dynamic_index_in_dim(array, self.mine, dim, keepdims=False)

    def other(self, array, dim):
        return lax.dynamic_index_in_dim(array, 1 - self.mine, dim, keepdims=False)

    def ordered(self, own, received, dim):
        low = jnp.where(self.mine == 0, own, received)
        high = jnp.where(self.mine == 0, received, own)
        return jnp.stack([low, high], dim)

    def gather(self, array, dim):
        return self.ordered(array, self.swap(array), dim)

    def exchange(self, array, split, dim):
        return self.ordered(self.own(array, split), self.swap(self.other(array, split)), dim)

    def reduce(self, array, split):
        received = self.swap(self.other(array, split))
        return self.own(array, split) + received


def make_local(n_dp, n_tensor):
    n_bits = n_dp.bit_length() - 1
    t_bits = n_tensor.bit_length() - 1

    def local(
        inputs,
        cotangent,
        gate_weight,
        up_weight,
        down_weight,
        gate_first,
        gate_second,
        up_first,
        up_second,
    ):
        bits = [Bit("dp", n_dp, place) for place in reversed(range(n_bits))]
        far, near, core = bits[0], bits[-2], bits[-1]
        middle = bits[1:-2]
        features = [Bit("tensor", n_tensor, place) for place in range(t_bits)]
        depth, columns = gate_weight.shape
        part = columns // 4
        chunks = CHUNKS if part % (CHUNKS * 128) == 0 else 1
        width = part // chunks

        def gather_features(block):
            for bit in features:
                block = bit.gather(block, 1).reshape(block.shape[0], 2 * block.shape[1])
            return block

        def gather_rows(block):
            return jnp.concatenate([block, near.swap(block)], 0)

        inputs_far, cotangent_far = far.swap(inputs), far.swap(cotangent)
        planes = [
            (gather_rows(gather_features(rows)), gather_features(gather_rows(cot)))
            for rows, cot in ((inputs, cotangent), (inputs_far, cotangent_far))
        ]

        weights = jnp.stack([gate_weight, up_weight, down_weight]).reshape(3, depth, 2, 2, part)
        weights = near.exchange(weights, 3, 1)

        def weights_of(chunk):
            piece = weights[..., chunk * width : (chunk + 1) * width]
            piece = far.exchange(piece, 3, 1)
            for done, bit in enumerate(middle):
                piece = bit.gather(piece, 2 + done)
            piece = core.gather(piece, piece.ndim - 2)
            return piece.reshape(3, n_dp * depth, width)

        def grads_of(piece):
            gate_up = jnp.concatenate([piece[0], piece[1]], 1)
            total = None
            for rows, cot in planes:
                sums = contract(rows, gate_up, 1)
                gate_sum, lift_sum = sums[:, :width], sums[:, width:]
                back_sum = contract(cot, piece[2], 1)
                sigmoid_gate = jax.nn.sigmoid(gate_sum)
                back_gate = back_sum * sigmoid_gate
                gate_rows = back_gate * lift_sum * (1.0 + gate_sum * (1.0 - sigmoid_gate))
                lift_rows = back_gate * gate_sum
                term = contract(rows, jnp.concatenate([gate_rows, lift_rows], 1), 0)
                total = term if total is None else total + term
            return total

        def scatter(total):
            grad = total.reshape([2] * n_bits + [depth, 2, width])
            grad = core.reduce(grad, n_bits - 1)
            for bit in middle:
                grad = bit.reduce(grad, 1)
            grad = far.exchange(grad, 0, 3)
            return near.exchange(grad, 0, 3)

        pieces = [scatter(grads_of(weights_of(chunk))) for chunk in range(chunks)]
        grads = jnp.stack(pieces, 4)
        gate_grad = grads[:, 0].reshape(depth, columns)
        lift_grad = grads[:, 1].reshape(depth, columns)
        gate_new, gate_first_new, gate_second_new = adam_update(
            gate_weight, gate_first, gate_second, gate_grad
        )
        up_new, up_first_new, up_second_new = adam_update(up_weight, up_first, up_second, lift_grad)
        return (gate_new, gate_first_new, gate_second_new, up_new, up_first_new, up_second_new)

    return local


def solution(mesh):
    spec = P("dp", "tensor")
    local = make_local(mesh.shape["dp"], mesh.shape["tensor"])
    return jax.shard_map(
        local, mesh=mesh, in_specs=(spec,) * 9, out_specs=(spec,) * 6, check_vma=False
    )
```

```python
import jax
import jax.numpy as jnp
from jax import lax
from jax.sharding import PartitionSpec as P

STEP = 100
CHUNKS = 4
PRECISION = lax.Precision.HIGH


def adam_update(weight, first, second, grad):
    first_new = 0.9 * first + 0.1 * grad
    second_new = 0.95 * second + 0.05 * grad * grad
    first_hat = first_new / (1.0 - 0.9**STEP)
    second_hat = second_new / (1.0 - 0.95**STEP)
    weight_new = weight - 0.003 * first_hat / (jnp.sqrt(second_hat) + 1e-08)
    return (weight_new, first_new, second_new)


def contract(left, right, left_dim):
    return lax.dot_general(
        left,
        right,
        (((left_dim,), (0,)), ((), ())),
        precision=PRECISION,
        preferred_element_type=jnp.float32,
    )


class Bit:
    def __init__(self, axis, size, place):
        self.axis = axis
        self.pairs = [(i, i ^ (1 << place)) for i in range(size)]
        self.mine = (lax.axis_index(axis) >> place) & 1

    def swap(self, array):
        return lax.ppermute(array, self.axis, self.pairs)

    def own(self, array, dim):
        return lax.dynamic_index_in_dim(array, self.mine, dim, keepdims=False)

    def other(self, array, dim):
        return lax.dynamic_index_in_dim(array, 1 - self.mine, dim, keepdims=False)

    def ordered(self, own, received, dim):
        low = jnp.where(self.mine == 0, own, received)
        high = jnp.where(self.mine == 0, received, own)
        return jnp.stack([low, high], dim)

    def joined(self, own, received, dim):
        low = jnp.where(self.mine == 0, own, received)
        high = jnp.where(self.mine == 0, received, own)
        return jnp.concatenate([low, high], dim)


def after(tree):
    leaves, shape = jax.tree.flatten(tree)
    return jax.tree.unflatten(shape, lax.optimization_barrier(leaves))


def make_local(n_dp, n_tensor):
    n_bits = n_dp.bit_length() - 1
    t_bits = n_tensor.bit_length() - 1

    def local(
        inputs,
        cotangent,
        gate_weight,
        up_weight,
        down_weight,
        gate_first,
        gate_second,
        up_first,
        up_second,
    ):
        bits = [Bit("dp", n_dp, place) for place in reversed(range(n_bits))]
        far, near, core = bits[0], bits[-2], bits[-1]
        middle = bits[1:-2]
        features = [Bit("tensor", n_tensor, place) for place in range(t_bits)]
        side, more = features[0], features[1:]
        depth, columns = gate_weight.shape
        part = columns // 4
        chunks = CHUNKS if part % (CHUNKS * 128) == 0 else 1
        width = part // chunks
        both = 2 * width
        half = (chunks + 1) // 2 * width

        def side_gather(block):
            return side.joined(block, side.swap(block), 1)

        def wide(own, received):
            block = side.joined(own, received, 1)
            for bit in more:
                block = bit.joined(block, bit.swap(block), 1)
            return block

        def columns_of(far_bit, near_bit):
            start = (far_bit * 2 + near_bit) * part
            return jnp.stack(
                [
                    lax.dynamic_slice_in_dim(weight, start, part, 1)
                    for weight in (gate_weight, up_weight, down_weight)
                ]
            )

        def over_middle(pair):
            moved = [pair]
            for bit in reversed(middle):
                moved = moved + [[bit.swap(x) for x in p] for p in moved]
            return moved

        def arranged(moved):
            blocks = [near.ordered(p[0], p[1], 0) for p in moved]
            for bit in middle:
                half_way = len(blocks) // 2
                blocks = [
                    bit.ordered(a, b, 0) for a, b in zip(blocks[:half_way], blocks[half_way:])
                ]
            return blocks[0].reshape((-1,) + blocks[0].shape[-3:])

        tokens = inputs.shape[0]
        n_features = inputs.shape[1] * n_tensor
        empty = jnp.zeros((4 * tokens, n_features), jnp.float32)

        def placed(rows, place, own, beside):
            return rows.at[place * tokens : (place + 1) * tokens].set(wide(own, beside))

        oo = columns_of(far.mine, near.mine)
        ox = columns_of(far.mine, 1 - near.mine)
        s = after(
            dict(
                in_far=far.swap(inputs),
                in_side=side.swap(inputs),
                cot_side=side.swap(cotangent),
                oo_near=near.swap(ox),
                in_near=near.swap(inputs),
                inputs=inputs,
                cotangent=cotangent,
                oo=oo,
                xo=columns_of(1 - far.mine, near.mine),
                xx=columns_of(1 - far.mine, 1 - near.mine),
                rows=empty,
                cots=empty,
            )
        )

        n_weight = 3 * depth
        by_near = jnp.concatenate([s["xx"].reshape(n_weight, part), s["cotangent"]], 0)
        by_near = near.swap(by_near)
        s = after(
            dict(
                s,
                cot_far=far.swap(s["cotangent"]),
                in_far_side=side.swap(s["in_far"]),
                in_diag=side.swap(s["in_near"]),
                xo_near=by_near[:n_weight].reshape(3, depth, part),
                cot_near=by_near[n_weight:],
                kept=over_middle([s["oo"]]),
                rows=placed(s["rows"], 0, s["inputs"], s["in_side"]),
                cots=placed(s["cots"], 0, s["cotangent"], s["cot_side"]),
            )
        )

        by_far = far.swap(jnp.stack([s["xo"][..., :half], s["xo_near"][..., :half]]))
        by_near = near.swap(jnp.concatenate([s["in_far"], s["cot_far"]], 0))
        rows = placed(s["rows"], 1, s["in_near"], s["in_diag"])
        s = after(
            dict(
                s,
                come=[by_far[0], by_far[1]],
                cot_diag=side.swap(s["cot_near"]),
                cot_far_side=side.swap(s["cot_far"]),
                in_far_near=by_near[:tokens],
                cot_far_near=by_near[tokens:],
                kept_near=over_middle([s["oo_near"]]),
                rows=placed(rows, 2, s["in_far"], s["in_far_side"]),
            )
        )

        late = None
        if half < part:
            late = far.swap(jnp.stack([s["xo"][..., half:], s["xo_near"][..., half:]]))
            late = [late[0], late[1]]
        kept = arranged([a + b for a, b in zip(s["kept"], s["kept_near"])])
        moved = jnp.stack(s["come"])
        come = over_middle([moved])
        come = arranged([[p[0][0], p[0][1]] for p in come])
        cots = placed(s["cots"], 1, s["cot_near"], s["cot_diag"])
        s = after(
            dict(
                s,
                late=late,
                in_far_diag=near.swap(s["in_far_side"]),
                cot_far_diag=side.swap(s["cot_far_near"]),
                kept=kept,
                kept_core=core.swap(kept),
                come=come,
                come_core=core.swap(come),
                cots=placed(cots, 2, s["cot_far"], s["cot_far_side"]),
            )
        )
        rows = placed(s["rows"], 3, s["in_far_near"], s["in_far_diag"])
        cots = placed(s["cots"], 3, s["cot_far_near"], s["cot_far_diag"])
        planes = [(rows, cots)]

        def weight_of(kept, kept_core, come, come_core):
            here = core.ordered(kept, kept_core, 1)
            there = core.ordered(come, come_core, 1)
            piece = far.ordered(here, there, 0)
            piece = jnp.moveaxis(piece, 3, 0)
            return piece.reshape(3, n_dp * depth, width)

        def grads_of(weight, planes):
            gate_up = jnp.concatenate([weight[0], weight[1]], 1)
            total = None
            for rows, cot in planes:
                sums = contract(rows, gate_up, 1)
                gate_sum, lift_sum = sums[:, :width], sums[:, width:]
                back_sum = contract(cot, weight[2], 1)
                sigmoid_gate = jax.nn.sigmoid(gate_sum)
                back_gate = back_sum * sigmoid_gate
                gate_rows = back_gate * lift_sum * (1.0 + gate_sum * (1.0 - sigmoid_gate))
                lift_rows = back_gate * gate_sum
                term = contract(rows, jnp.concatenate([gate_rows, lift_rows], 1), 0)
                total = term if total is None else total + term
            return total.reshape([2] * n_bits + [depth, both])

        kept, kept_core = s["kept"], s["kept_core"]
        arrived = {0: (s["come"], s["come_core"])}
        late = s["late"]
        stages = {}
        for step in range(chunks + 4):
            new = {}
            if step - 3 >= 0 and step - 3 < chunks:
                keep, send = stages[step - 3]
                new[step - 3] = near.ordered(keep, near.swap(send), 0)
            if step - 2 >= 0 and step - 2 < chunks:
                keep, send = stages[step - 2]
                grad = far.ordered(keep, far.swap(send), 1)
                new[step - 2] = (near.own(grad, 0), near.other(grad, 0))
            if step - 1 >= 0 and step - 1 < chunks:
                grad = stages[step - 1]
                for bit in middle:
                    grad = bit.own(grad, 1) + bit.swap(bit.other(grad, 1))
                new[step - 1] = (far.own(grad, 0), far.other(grad, 0))
            if step < chunks:
                group, start = (0, step * width) if step * width < half else (1, step * width - half)
                cuts = [x[..., step * width : (step + 1) * width] for x in (kept, kept_core)]
                cuts += [x[..., start : start + width] for x in arrived[group]]
                grad = grads_of(weight_of(*cuts), planes)
                send = core.other(grad, n_bits - 1)
                new[step] = core.own(grad, n_bits - 1) + core.swap(send)
            fresh = None
            if step == 0 and late is not None:
                fresh = over_middle([jnp.stack(late)])
                fresh = arranged([[p[0][0], p[0][1]] for p in fresh])
                fresh = (fresh, core.swap(fresh))
            stages.update(new)
            if step < chunks + 3:
                stages, kept, kept_core, planes, fresh, arrived = after(
                    (stages, kept, kept_core, planes, fresh, arrived)
                )
            if step == 0 and late is not None:
                arrived[1] = fresh

        def assembled(which):
            return jnp.concatenate(
                [
                    stages[chunk][n, f, :, which * width : (which + 1) * width]
                    for f in range(2)
                    for n in range(2)
                    for chunk in range(chunks)
                ],
                1,
            )

        gate_new, gate_first_new, gate_second_new = adam_update(
            gate_weight, gate_first, gate_second, assembled(0)
        )
        up_new, up_first_new, up_second_new = adam_update(
            up_weight, up_first, up_second, assembled(1)
        )
        return (gate_new, gate_first_new, gate_second_new, up_new, up_first_new, up_second_new)

    return local


def solution(mesh):
    spec = P("dp", "tensor")
    local = make_local(mesh.shape["dp"], mesh.shape["tensor"])
    return jax.shard_map(
        local, mesh=mesh, in_specs=(spec,) * 9, out_specs=(spec,) * 6, check_vma=False
    )
```

```python
import functools

import jax
import jax.numpy as jnp
from jax import lax
from jax.experimental import pallas as pl
from jax.experimental.pallas import tpu as pltpu
from jax.sharding import PartitionSpec as P

STEP = 100
CHUNKS = 4
VMEM_LIMIT = 60 * 1024 * 1024


def adam_update(weight, first, second, grad):
    first_new = 0.9 * first + 0.1 * grad
    second_new = 0.95 * second + 0.05 * grad * grad
    first_hat = first_new / (1.0 - 0.9**STEP)
    second_hat = second_new / (1.0 - 0.95**STEP)
    weight_new = weight - 0.003 * first_hat / (jnp.sqrt(second_hat) + 1e-08)
    return (weight_new, first_new, second_new)


class Bit:
    def __init__(self, axis, size, place):
        self.axis = axis
        self.pairs = [(i, i ^ (1 << place)) for i in range(size)]
        self.mine = (lax.axis_index(axis) >> place) & 1

    def swap(self, array):
        return lax.ppermute(array, self.axis, self.pairs)

    def own(self, array, dim):
        return lax.dynamic_index_in_dim(array, self.mine, dim, keepdims=False)

    def other(self, array, dim):
        return lax.dynamic_index_in_dim(array, 1 - self.mine, dim, keepdims=False)

    def ordered(self, own, received, dim):
        low = jnp.where(self.mine == 0, own, received)
        high = jnp.where(self.mine == 0, received, own)
        return jnp.stack([low, high], dim)

    def joined(self, own, received, dim):
        low = jnp.where(self.mine == 0, own, received)
        high = jnp.where(self.mine == 0, received, own)
        return jnp.concatenate([low, high], dim)


def parts_of(x):
    high = x.astype(jnp.bfloat16)
    return high, (x - high.astype(jnp.float32)).astype(jnp.bfloat16)


def product(left, right, left_dim):
    dims = (((left_dim,), (0,)), ((), ()))
    dot = functools.partial(
        lax.dot_general, dimension_numbers=dims, preferred_element_type=jnp.float32
    )
    return dot(left[0], right[0]) + (dot(left[0], right[1]) + dot(left[1], right[0]))


def chunk_kernel(starts, width, mine_ref, *refs):
    sources, (keep_ref, send_ref) = refs[:20], refs[20:22]
    held, piece, up_high, up_low, down_high, down_low, total, done = refs[22:]
    side, core, far = mine_ref[0], mine_ref[1], mine_ref[2]
    _, blocks, _, depth, _ = piece.shape
    half = held.shape[2]

    copies = []
    for i, start in enumerate(starts):
        source = sources[16 + i].at[:, :, :, pl.ds(start, width)]
        copies.append(pltpu.make_async_copy(source, piece.at[i], done.at[i]))
    for b in range(4):
        for i in (2 * b, 2 * b + 1, 8 + 2 * b, 9 + 2 * b):
            copies.append(pltpu.make_async_copy(sources[i], held.at[i], done.at[4 + i]))
    for copy in copies:
        copy.start()

    for i, (place, bit) in enumerate(
        ((far, core), (far, 1 - core), (1 - far, core), (1 - far, 1 - core))
    ):
        copies[i].wait()
        for block in range(blocks):
            row = pl.multiple_of(((place * blocks + block) * 2 + bit) * depth, depth)
            for k in range(3):
                high, low = parts_of(piece[i, block, k])
                if k < 2:
                    up_high[pl.ds(row, depth), k * width : (k + 1) * width] = high
                    up_low[pl.ds(row, depth), k * width : (k + 1) * width] = low
                else:
                    down_high[pl.ds(row, depth), :] = high
                    down_low[pl.ds(row, depth), :] = low

    at = [pl.ds(pl.multiple_of(h * half, half), half) for h in (side, 1 - side)]
    for b in range(4):
        for copy in copies[4 + 4 * b : 8 + 4 * b]:
            copy.wait()
        pieces = [parts_of(held[2 * b + h]) for h in range(2)]
        sums = sum(product(pieces[h], (up_high[at[h], :], up_low[at[h], :]), 1) for h in range(2))
        back = sum(
            product(
                parts_of(held[8 + 2 * b + h]), (down_high[at[h], :], down_low[at[h], :]), 1
            )
            for h in range(2)
        )
        gate, lift = sums[:, :width], sums[:, width:]
        sigmoid = 1.0 / (1.0 + jnp.exp(-gate))
        back = back * sigmoid
        grads = parts_of(
            jnp.concatenate([back * lift * (1.0 + gate * (1.0 - sigmoid)), back * gate], 1)
        )
        for h in range(2):
            term = product(grads, pieces[h], 0)
            total[h] = term if b == 0 else total[h] + term

    for h, place in ((0, side), (1, 1 - side)):
        turned = total[h].T
        for bit in range(2):
            for ref, whose in ((keep_ref, bit), (send_ref, 1 - bit)):

                @pl.when(core == whose)
                def _():
                    for block in range(blocks):
                        start = (block * 2 + bit) * depth
                        ref[place * blocks + block] = turned[start : start + depth, :]


def after(tree):
    leaves, shape = jax.tree.flatten(tree)
    return jax.tree.unflatten(shape, lax.optimization_barrier(leaves))


def make_local(n_dp, n_tensor):
    n_bits = n_dp.bit_length() - 1
    t_bits = n_tensor.bit_length() - 1

    def local(
        inputs,
        cotangent,
        gate_weight,
        up_weight,
        down_weight,
        gate_first,
        gate_second,
        up_first,
        up_second,
    ):
        bits = [Bit("dp", n_dp, place) for place in reversed(range(n_bits))]
        far, near, core = bits[0], bits[-2], bits[-1]
        middle = bits[1:-2]
        features = [Bit("tensor", n_tensor, place) for place in range(t_bits)]
        side = features[-1]
        depth, columns = gate_weight.shape
        part = columns // 4
        chunks = CHUNKS if part % (CHUNKS * 128) == 0 else 1
        width = part // chunks
        both = 2 * width
        half = (chunks + 1) // 2 * width
        most = (chunks - chunks // 4) * width
        for bit in features[:-1]:
            inputs = bit.joined(inputs, bit.swap(inputs), 1)
            cotangent = bit.joined(cotangent, bit.swap(cotangent), 1)

        def columns_of(far_bit, near_bit):
            start = (far_bit * 2 + near_bit) * part
            return jnp.stack(
                [
                    lax.dynamic_slice_in_dim(weight, start, part, 1)
                    for weight in (gate_weight, up_weight, down_weight)
                ]
            )

        def over_middle(pair):
            moved = [pair]
            for bit in reversed(middle):
                moved = moved + [[bit.swap(x) for x in p] for p in moved]
            return moved

        def arranged(moved):
            blocks = [near.ordered(p[0], p[1], 0) for p in moved]
            for bit in middle:
                half_way = len(blocks) // 2
                blocks = [
                    bit.ordered(a, b, 0) for a, b in zip(blocks[:half_way], blocks[half_way:])
                ]
            return blocks[0].reshape((-1,) + blocks[0].shape[-3:])

        tokens = inputs.shape[0]

        oo = columns_of(far.mine, near.mine)
        ox = columns_of(far.mine, 1 - near.mine)
        s = after(
            dict(
                in_far=far.swap(inputs),
                in_side=side.swap(inputs),
                cot_side=side.swap(cotangent),
                oo_near=near.swap(ox),
                in_near=near.swap(inputs),
                inputs=inputs,
                cotangent=cotangent,
                oo=oo,
                xo=columns_of(1 - far.mine, near.mine),
                xx=columns_of(1 - far.mine, 1 - near.mine),
            )
        )

        n_weight = 3 * depth * part // cotangent.shape[1]
        by_near = jnp.concatenate([s["xx"].reshape(n_weight, -1), s["cotangent"]], 0)
        by_near = near.swap(by_near)
        s = after(
            dict(
                s,
                cot_far=far.swap(s["cotangent"]),
                in_far_side=side.swap(s["in_far"]),
                in_diag=side.swap(s["in_near"]),
                xo_near=by_near[:n_weight].reshape(3, depth, part),
                cot_near=by_near[n_weight:],
                kept=over_middle([s["oo"]]),
            )
        )

        by_far = far.swap(jnp.stack([s["xo"][..., :most], s["xo_near"][..., :most]]))
        by_near = near.swap(jnp.concatenate([s["in_far"], s["cot_far"]], 0))
        s = after(
            dict(
                s,
                come=by_far,
                send=jnp.stack([s["xo"][..., most:], s["xo_near"][..., most:]]),
                cot_diag=side.swap(s["cot_near"]),
                cot_far_side=side.swap(s["cot_far"]),
                in_far_near=by_near[:tokens],
                cot_far_near=by_near[tokens:],
                kept_near=over_middle([s["oo_near"]]),
            )
        )

        late = s["come"][..., half:]
        if most < part:
            late = (late, far.swap(s["send"]))
        kept = arranged([a + b for a, b in zip(s["kept"], s["kept_near"])])
        s = after(
            dict(
                s,
                late=late,
                in_far_diag=near.swap(s["in_far_side"]),
                cot_far_diag=side.swap(s["cot_far_near"]),
                kept=kept,
                kept_core=core.swap(kept),
                come=over_middle([s["come"][..., :half]]),
            )
        )
        come = arranged([[p[0][0], p[0][1]] for p in s["come"]])
        s = after(dict(s, come=come, come_core=core.swap(come)))
        tokens_of = [
            s[name]
            for name in (
                "inputs", "in_side", "in_near", "in_diag",
                "in_far", "in_far_side", "in_far_near", "in_far_diag",
                "cotangent", "cot_side", "cot_near", "cot_diag",
                "cot_far", "cot_far_side", "cot_far_near", "cot_far_diag",
            )
        ]
        mine = jnp.stack([side.mine, core.mine, far.mine]).astype(jnp.int32)

        def grads_of(ahead, kept_at, come_at, *arrays):
            feature_rows = n_dp * depth
            out = jax.ShapeDtypeStruct((n_dp // 2, depth, both), jnp.float32)
            vmem = pl.BlockSpec(memory_space=pltpu.VMEM)
            any_space = pl.BlockSpec(memory_space=pl.ANY)
            starts = (kept_at, kept_at, come_at, come_at)
            keep, send = pl.pallas_call(
                functools.partial(chunk_kernel, starts, width),
                out_shape=(out, out),
                in_specs=[pl.BlockSpec(memory_space=pltpu.SMEM)] + [any_space] * len(arrays),
                out_specs=(vmem, vmem),
                scratch_shapes=[
                    pltpu.VMEM((16,) + inputs.shape, jnp.float32),
                    pltpu.VMEM((4, n_dp // 4, 3, depth, width), jnp.float32),
                    pltpu.VMEM((feature_rows, both), jnp.bfloat16),
                    pltpu.VMEM((feature_rows, both), jnp.bfloat16),
                    pltpu.VMEM((feature_rows, width), jnp.bfloat16),
                    pltpu.VMEM((feature_rows, width), jnp.bfloat16),
                    pltpu.VMEM((2, both, feature_rows // 2), jnp.float32),
                    pltpu.SemaphoreType.DMA((20,)),
                ],
                compiler_params=pltpu.CompilerParams(vmem_limit_bytes=VMEM_LIMIT),
                cost_estimate=pl.CostEstimate(
                    flops=24 * tokens * feature_rows * 5 * width // 2,
                    bytes_accessed=16 * tokens * feature_rows,
                    transcendentals=4 * tokens * width,
                ),
            )(mine, *arrays)
            shape = [2] * (n_bits - 1) + [depth, both]
            send, ahead = after((send, ahead))
            return (keep.reshape(shape), core.swap(send).reshape(shape)), ahead

        kept, kept_core = s["kept"], s["kept_core"]
        arrived = {0: (s["come"], s["come_core"])}
        late = s["late"]
        stages = {}
        fresh = None
        for step in range(chunks + 4):
            new = {}
            if step - 3 >= 0 and step - 3 < chunks:
                keep, send = stages[step - 3]
                new[step - 3] = near.ordered(keep, near.swap(send), 0)
            if step - 2 >= 0 and step - 2 < chunks:
                keep, send = stages[step - 2]
                grad = far.ordered(keep, far.swap(send), 1)
                new[step - 2] = (near.own(grad, 0), near.other(grad, 0))
            if step - 1 >= 0 and step - 1 < chunks:
                terms = stages[step - 1]
                for bit in middle:
                    keep, send = (sum(part(x, 1) for x in terms) for part in (bit.own, bit.other))
                    terms = (keep, bit.swap(send))
                grad = sum(terms)
                new[step - 1] = (far.own(grad, 0), far.other(grad, 0))
            if step == 0 and half < part:
                fresh = over_middle([jnp.concatenate(late, -1) if most < part else late])
            if step == 1 and half < part:
                fresh = arranged([[p[0][0], p[0][1]] for p in fresh])
                fresh = (fresh, core.swap(fresh))
            if step < chunks:
                group, start = (0, step * width) if step * width < half else (1, step * width - half)
                new[step], fresh = grads_of(
                    fresh, step * width, start, *tokens_of, kept, kept_core, *arrived[group]
                )
            stages.update(new)
            if step < chunks + 3:
                stages, kept, kept_core, tokens_of, fresh, arrived = after(
                    (stages, kept, kept_core, tokens_of, fresh, arrived)
                )
            if step == 1 and half < part:
                arrived[1] = fresh

        def assembled(which):
            return jnp.concatenate(
                [
                    stages[chunk][n, f, :, which * width : (which + 1) * width]
                    for f in range(2)
                    for n in range(2)
                    for chunk in range(chunks)
                ],
                1,
            )

        gate_new, gate_first_new, gate_second_new = adam_update(
            gate_weight, gate_first, gate_second, assembled(0)
        )
        up_new, up_first_new, up_second_new = adam_update(
            up_weight, up_first, up_second, assembled(1)
        )
        return (gate_new, gate_first_new, gate_second_new, up_new, up_first_new, up_second_new)

    return local


def solution(mesh):
    spec = P("dp", "tensor")
    local = make_local(mesh.shape["dp"], mesh.shape["tensor"])
    return jax.shard_map(
        local, mesh=mesh, in_specs=(spec,) * 9, out_specs=(spec,) * 6, check_vma=False
    )
```

```python
import functools

import jax
import jax.numpy as jnp
from jax import lax
from jax.experimental import pallas as pl
from jax.experimental.pallas import tpu as pltpu
from jax.sharding import PartitionSpec as P

STEP = 100
CHUNKS = 4
VMEM_LIMIT = 60 * 1024 * 1024


def adam_update(weight, first, second, grad):
    first_new = 0.9 * first + 0.1 * grad
    second_new = 0.95 * second + 0.05 * grad * grad
    first_hat = first_new / (1.0 - 0.9**STEP)
    second_hat = second_new / (1.0 - 0.95**STEP)
    weight_new = weight - 0.003 * first_hat / (jnp.sqrt(second_hat) + 1e-08)
    return (weight_new, first_new, second_new)


class Bit:
    def __init__(self, axis, size, place):
        self.axis = axis
        self.pairs = [(i, i ^ (1 << place)) for i in range(size)]
        self.mine = (lax.axis_index(axis) >> place) & 1

    def swap(self, array):
        return lax.ppermute(array, self.axis, self.pairs)

    def own(self, array, dim):
        return lax.dynamic_index_in_dim(array, self.mine, dim, keepdims=False)

    def other(self, array, dim):
        return lax.dynamic_index_in_dim(array, 1 - self.mine, dim, keepdims=False)

    def ordered(self, own, received, dim):
        low = jnp.where(self.mine == 0, own, received)
        high = jnp.where(self.mine == 0, received, own)
        return jnp.stack([low, high], dim)

    def joined(self, own, received, dim):
        low = jnp.where(self.mine == 0, own, received)
        high = jnp.where(self.mine == 0, received, own)
        return jnp.concatenate([low, high], dim)


def parts_of(x):
    high = x.astype(jnp.bfloat16)
    return high, (x - high.astype(jnp.float32)).astype(jnp.bfloat16)


def product(left, right, left_dim):
    dims = (((left_dim,), (0,)), ((), ()))
    dot = functools.partial(
        lax.dot_general, dimension_numbers=dims, preferred_element_type=jnp.float32
    )
    return dot(left[0], right[0]) + (dot(left[0], right[1]) + dot(left[1], right[0]))


def chunk_kernel(starts, width, mine_ref, *refs):
    sources, (keep_ref, send_ref) = refs[:20], refs[20:22]
    held, piece, up_high, up_low, down_high, down_low = refs[22:28]
    high_rows, low_rows, high_grads, low_grads, total, done = refs[28:]
    side, core, far = mine_ref[0], mine_ref[1], mine_ref[2]
    _, blocks, _, depth, _ = piece.shape
    tokens, half = held.shape[1:]
    units = keep_ref.shape[0]
    unit = width // units

    copies = []
    for i, start in enumerate(starts):
        source = sources[16 + i].at[:, :, :, pl.ds(start, width)]
        copies.append(pltpu.make_async_copy(source, piece.at[i], done.at[i]))
    for b in range(4):
        for i in (2 * b, 2 * b + 1, 8 + 2 * b, 9 + 2 * b):
            copies.append(pltpu.make_async_copy(sources[i], held.at[i], done.at[4 + i]))
    for copy in copies:
        copy.start()

    for i, (place, bit) in enumerate(
        ((far, core), (far, 1 - core), (1 - far, core), (1 - far, 1 - core))
    ):
        copies[i].wait()
        for block in range(blocks):
            row = pl.multiple_of(((place * blocks + block) * 2 + bit) * depth, depth)
            for k in range(3):
                high, low = parts_of(piece[i, block, k])
                if k < 2:
                    up_high[pl.ds(row, depth), k * width : (k + 1) * width] = high
                    up_low[pl.ds(row, depth), k * width : (k + 1) * width] = low
                else:
                    down_high[pl.ds(row, depth), :] = high
                    down_low[pl.ds(row, depth), :] = low

    at = [pl.ds(pl.multiple_of(h * half, half), half) for h in (side, 1 - side)]
    for b in range(4):
        for copy in copies[4 + 4 * b : 8 + 4 * b]:
            copy.wait()
        here = slice(b * tokens, (b + 1) * tokens)
        pieces = [parts_of(held[2 * b + h]) for h in range(2)]
        for h in range(2):
            high_rows[h, here], low_rows[h, here] = pieces[h]
        sums = sum(product(pieces[h], (up_high[at[h], :], up_low[at[h], :]), 1) for h in range(2))
        back = sum(
            product(parts_of(held[8 + 2 * b + h]), (down_high[at[h], :], down_low[at[h], :]), 1)
            for h in range(2)
        )
        gate, lift = sums[:, :width], sums[:, width:]
        sigmoid = 1.0 / (1.0 + jnp.exp(-gate))
        back = back * sigmoid
        gate, lift = back * lift * (1.0 + gate * (1.0 - sigmoid)), back * gate
        grads = [x[:, u * unit : (u + 1) * unit] for u in range(units) for x in (gate, lift)]
        high_grads[here], low_grads[here] = parts_of(jnp.concatenate(grads, 1))
        if b % 2 == 1:
            pair = slice((b - 1) * tokens, (b + 1) * tokens)
            for h in range(2):
                term = product(
                    (high_rows[h, pair], low_rows[h, pair]),
                    (high_grads[pair], low_grads[pair]),
                    0,
                )
                total[h] = term if b == 1 else total[h] + term

    for h, place in ((0, side), (1, 1 - side)):
        for u in range(units):
            for bit in range(2):
                for ref, whose in ((keep_ref, bit), (send_ref, 1 - bit)):

                    @pl.when(core == whose)
                    def _():
                        for block in range(blocks):
                            start = (block * 2 + bit) * depth
                            ref[u, place * blocks + block] = total[
                                h, start : start + depth, u * 2 * unit : (u + 1) * 2 * unit
                            ]


def after(tree):
    leaves, shape = jax.tree.flatten(tree)
    return jax.tree.unflatten(shape, lax.optimization_barrier(leaves))


def make_local(n_dp, n_tensor):
    n_bits = n_dp.bit_length() - 1
    t_bits = n_tensor.bit_length() - 1

    def local(
        inputs,
        cotangent,
        gate_weight,
        up_weight,
        down_weight,
        gate_first,
        gate_second,
        up_first,
        up_second,
    ):
        bits = [Bit("dp", n_dp, place) for place in reversed(range(n_bits))]
        far, near, core = bits[0], bits[-2], bits[-1]
        middle = bits[1:-2]
        features = [Bit("tensor", n_tensor, place) for place in range(t_bits)]
        side = features[-1]
        depth, columns = gate_weight.shape
        part = columns // 4
        chunks = CHUNKS if part % (CHUNKS * 128) == 0 else 1
        width = part // chunks
        both = 2 * width
        sizes = [chunks // 2] + [1] * (chunks // 2) if chunks % 2 == 0 else [chunks]
        half = sizes[0] * width
        most = (chunks - chunks // 4) * width
        for bit in features[:-1]:
            inputs = bit.joined(inputs, bit.swap(inputs), 1)
            cotangent = bit.joined(cotangent, bit.swap(cotangent), 1)

        def columns_of(far_bit, near_bit):
            start = (far_bit * 2 + near_bit) * part
            return jnp.stack(
                [
                    lax.dynamic_slice_in_dim(weight, start, part, 1)
                    for weight in (gate_weight, up_weight, down_weight)
                ]
            )

        def over_middle(pair):
            moved = [pair]
            for bit in reversed(middle):
                moved = moved + [[bit.swap(x) for x in p] for p in moved]
            return moved

        def arranged(moved):
            blocks = [near.ordered(p[0], p[1], 0) for p in moved]
            for bit in middle:
                half_way = len(blocks) // 2
                blocks = [
                    bit.ordered(a, b, 0) for a, b in zip(blocks[:half_way], blocks[half_way:])
                ]
            return blocks[0].reshape((-1,) + blocks[0].shape[-3:])

        tokens = inputs.shape[0]

        pairs = [(i, i ^ (1 << (n_bits - 1)) ^ 2) for i in range(n_dp)]

        def diagonal(array):
            return lax.ppermute(array, "dp", pairs)

        oo = columns_of(far.mine, near.mine)
        ox = columns_of(far.mine, 1 - near.mine)
        s = after(
            dict(
                in_far=far.swap(inputs),
                in_side=side.swap(inputs),
                cot_side=side.swap(cotangent),
                oo_near=near.swap(ox),
                in_near=near.swap(inputs),
                inputs=inputs,
                cotangent=cotangent,
                oo=oo,
                xo=columns_of(1 - far.mine, near.mine),
                xx=columns_of(1 - far.mine, 1 - near.mine),
            )
        )

        n_weight = 3 * depth * part // cotangent.shape[1]
        by_near = jnp.concatenate([s["xx"].reshape(n_weight, -1), s["cotangent"]], 0)
        by_near = near.swap(by_near)
        s = after(
            dict(
                s,
                cot_far=far.swap(s["cotangent"]),
                in_far_side=side.swap(s["in_far"]),
                in_diag=side.swap(s["in_near"]),
                xo_near=by_near[:n_weight].reshape(3, depth, part),
                cot_near=by_near[n_weight:],
                kept=over_middle([s["oo"]]),
            )
        )

        by_far = far.swap(jnp.stack([s["xo"][..., :most], s["xo_near"][..., :most]]))
        by_near = near.swap(jnp.concatenate([s["in_far"], s["cot_far"]], 0))
        s = after(
            dict(
                s,
                come=by_far,
                send=jnp.stack([s["xo"][..., most:], s["xo_near"][..., most:]]),
                cot_diag=side.swap(s["cot_near"]),
                cot_far_side=side.swap(s["cot_far"]),
                in_far_near=by_near[:tokens],
                cot_far_near=by_near[tokens:],
                kept_near=over_middle([s["oo_near"]]),
            )
        )

        late = s["come"][..., half:]
        if most < part:
            late = (late, far.swap(s["send"]))
        kept = arranged([a + b for a, b in zip(s["kept"], s["kept_near"])])
        s = after(
            dict(
                s,
                late=late,
                in_far_diag=near.swap(s["in_far_side"]),
                cot_far_diag=side.swap(s["cot_far_near"]),
                kept=kept,
                kept_core=core.swap(kept),
                come=over_middle([s["come"][..., :half]]),
            )
        )
        come = arranged([[p[0][0], p[0][1]] for p in s["come"]])
        s = after(dict(s, come=come, come_core=core.swap(come)))
        tokens_of = [
            s[name]
            for name in (
                "inputs", "in_side", "in_near", "in_diag",
                "in_far", "in_far_side", "in_far_near", "in_far_diag",
                "cotangent", "cot_side", "cot_near", "cot_diag",
                "cot_far", "cot_far_side", "cot_far_near", "cot_far_diag",
            )
        ]
        mine = jnp.stack([side.mine, core.mine, far.mine]).astype(jnp.int32)

        def grads_of(ahead, units, kept_at, come_at, *arrays):
            held = units * width
            feature_rows = n_dp * depth
            out = jax.ShapeDtypeStruct((units, n_dp // 2, depth, both), jnp.float32)
            vmem = pl.BlockSpec(memory_space=pltpu.VMEM)
            any_space = pl.BlockSpec(memory_space=pl.ANY)
            all_tokens = 4 * tokens
            keep, send = pl.pallas_call(
                functools.partial(chunk_kernel, (kept_at, kept_at, come_at, come_at), held),
                out_shape=(out, out),
                in_specs=[pl.BlockSpec(memory_space=pltpu.SMEM)] + [any_space] * len(arrays),
                out_specs=(vmem, vmem),
                scratch_shapes=[
                    pltpu.VMEM((16,) + inputs.shape, jnp.float32),
                    pltpu.VMEM((4, n_dp // 4, 3, depth, held), jnp.float32),
                    pltpu.VMEM((feature_rows, 2 * held), jnp.bfloat16),
                    pltpu.VMEM((feature_rows, 2 * held), jnp.bfloat16),
                    pltpu.VMEM((feature_rows, held), jnp.bfloat16),
                    pltpu.VMEM((feature_rows, held), jnp.bfloat16),
                    pltpu.VMEM((2, all_tokens, feature_rows // 2), jnp.bfloat16),
                    pltpu.VMEM((2, all_tokens, feature_rows // 2), jnp.bfloat16),
                    pltpu.VMEM((all_tokens, 2 * held), jnp.bfloat16),
                    pltpu.VMEM((all_tokens, 2 * held), jnp.bfloat16),
                    pltpu.VMEM((2, feature_rows // 2, 2 * held), jnp.float32),
                    pltpu.SemaphoreType.DMA((20,)),
                ],
                compiler_params=pltpu.CompilerParams(vmem_limit_bytes=VMEM_LIMIT),
                cost_estimate=pl.CostEstimate(
                    flops=30 * all_tokens * feature_rows * held,
                    bytes_accessed=8 * all_tokens * feature_rows,
                    transcendentals=all_tokens * held,
                ),
            )(mine, *arrays)
            shape = [units] + [2] * (n_bits - 1) + [depth, both]
            send, ahead = after((send, ahead))
            return [keep.reshape(shape), core.swap(send).reshape(shape)], ahead

        kept, kept_core = s["kept"], s["kept_core"]
        arrived = (s["come"], s["come_core"])
        late = s["late"]
        calls = len(sizes)
        firsts = [sum(sizes[:call]) for call in range(calls)]
        stages = {}
        for step in range(calls + 2):
            new = {}
            for call in range(calls):
                if step == call + 2:
                    own, beside, beyond, across = stages[call]
                    own = near.ordered(own, near.swap(beside), 1)
                    beyond = near.ordered(far.swap(beyond), diagonal(across), 1)
                    new[call] = far.ordered(own, beyond, 2)
                if step == call + 1:
                    terms = stages[call]
                    for bit in middle:
                        keep, send = (
                            sum(part(x, 2) for x in terms) for part in (bit.own, bit.other)
                        )
                        terms = [keep, bit.swap(send)]
                    new[call] = [
                        sum(there(here(x, 1), 1) for x in terms)
                        for here in (far.own, far.other)
                        for there in (near.own, near.other)
                    ]
            if step < calls:
                fresh = None
                if step == 0 and calls > 1:
                    fresh = over_middle([jnp.concatenate(late, -1) if most < part else late])
                come_at = max(firsts[step] * width - half, 0)
                terms, (fresh, new) = grads_of(
                    (fresh, new), sizes[step], firsts[step] * width, come_at,
                    *tokens_of, kept, kept_core, *arrived,
                )
                new[step] = terms
                if step == 0 and calls > 1:
                    fresh = arranged([[p[0][0], p[0][1]] for p in fresh])
                    arrived = (fresh, core.swap(fresh))
            stages.update(new)
            if step < calls + 1:
                stages, kept, kept_core, tokens_of, arrived = after(
                    (stages, kept, kept_core, tokens_of, arrived)
                )

        pieces = []
        for call in range(calls):
            pieces += [stages[call][u] for u in range(sizes[call])]

        def assembled(which):
            return jnp.concatenate(
                [
                    pieces[chunk][n, f, :, which * width : (which + 1) * width]
                    for f in range(2)
                    for n in range(2)
                    for chunk in range(chunks)
                ],
                1,
            )

        gate_new, gate_first_new, gate_second_new = adam_update(
            gate_weight, gate_first, gate_second, assembled(0)
        )
        up_new, up_first_new, up_second_new = adam_update(
            up_weight, up_first, up_second, assembled(1)
        )
        return (gate_new, gate_first_new, gate_second_new, up_new, up_first_new, up_second_new)

    return local


def solution(mesh):
    spec = P("dp", "tensor")
    local = make_local(mesh.shape["dp"], mesh.shape["tensor"])
    return jax.shard_map(
        local, mesh=mesh, in_specs=(spec,) * 9, out_specs=(spec,) * 6, check_vma=False
    )
```

```python
import functools

import jax
import jax.numpy as jnp
from jax import lax
from jax.experimental import pallas as pl
from jax.experimental.pallas import tpu as pltpu
from jax.sharding import PartitionSpec as P

STEP = 100
CHUNKS = 4
VMEM_LIMIT = 52 * 1024 * 1024


def adam_update(weight, first, second, grad):
    first_new = 0.9 * first + 0.1 * grad
    second_new = 0.95 * second + 0.05 * grad * grad
    first_hat = first_new / (1.0 - 0.9**STEP)
    second_hat = second_new / (1.0 - 0.95**STEP)
    weight_new = weight - 0.003 * first_hat / (jnp.sqrt(second_hat) + 1e-08)
    return (weight_new, first_new, second_new)


class Bit:
    def __init__(self, axis, size, place):
        self.axis = axis
        self.pairs = [(i, i ^ (1 << place)) for i in range(size)]
        self.mine = (lax.axis_index(axis) >> place) & 1

    def swap(self, array):
        return lax.ppermute(array, self.axis, self.pairs)

    def own(self, array, dim):
        return lax.dynamic_index_in_dim(array, self.mine, dim, keepdims=False)

    def other(self, array, dim):
        return lax.dynamic_index_in_dim(array, 1 - self.mine, dim, keepdims=False)

    def ordered(self, own, received, dim):
        low = jnp.where(self.mine == 0, own, received)
        high = jnp.where(self.mine == 0, received, own)
        return jnp.stack([low, high], dim)

    def joined(self, own, received, dim):
        low = jnp.where(self.mine == 0, own, received)
        high = jnp.where(self.mine == 0, received, own)
        return jnp.concatenate([low, high], dim)


def parts_of(x):
    high = x.astype(jnp.bfloat16)
    return high, (x - high.astype(jnp.float32)).astype(jnp.bfloat16)


def product(left, right, left_dim):
    dims = (((left_dim,), (0,)), ((), ()))
    dot = functools.partial(
        lax.dot_general, dimension_numbers=dims, preferred_element_type=jnp.float32
    )
    return dot(left[0], right[0]) + (dot(left[0], right[1]) + dot(left[1], right[0]))


def chunk_kernel(starts, width, mine_ref, *refs):
    sources, (keep_ref, send_ref) = refs[:20], refs[20:22]
    held, piece, up_high, up_low, down_high, down_low = refs[22:28]
    high_rows, low_rows, high_grads, low_grads, total, done = refs[28:]
    side, core, far = mine_ref[0], mine_ref[1], mine_ref[2]
    _, blocks, _, depth, _ = piece.shape
    tokens, half = held.shape[1:]
    units = keep_ref.shape[0]
    unit = width // units

    copies = []
    for i, start in enumerate(starts):
        source = sources[16 + i].at[:, :, :, pl.ds(start, width)]
        copies.append(pltpu.make_async_copy(source, piece.at[i], done.at[i]))
    for b in range(4):
        for i in (2 * b, 2 * b + 1, 8 + 2 * b, 9 + 2 * b):
            copies.append(pltpu.make_async_copy(sources[i], held.at[i], done.at[4 + i]))
    for copy in copies[:8]:
        copy.start()

    for i, (place, bit) in enumerate(
        ((far, core), (far, 1 - core), (1 - far, core), (1 - far, 1 - core))
    ):
        copies[i].wait()
        for block in range(blocks):
            row = pl.multiple_of(((place * blocks + block) * 2 + bit) * depth, depth)
            for k in range(3):
                high, low = parts_of(piece[i, block, k])
                if k < 2:
                    up_high[pl.ds(row, depth), k * width : (k + 1) * width] = high
                    up_low[pl.ds(row, depth), k * width : (k + 1) * width] = low
                else:
                    down_high[pl.ds(row, depth), :] = high
                    down_low[pl.ds(row, depth), :] = low

    for copy in copies[8:12]:
        copy.start()
    at = [pl.ds(pl.multiple_of(h * half, half), half) for h in (side, 1 - side)]
    for b in range(4):
        for copy in copies[4 + 4 * b : 8 + 4 * b]:
            copy.wait()
        for copy in copies[12 + 4 * b : 16 + 4 * b]:
            copy.start()
        here = slice(b * tokens, (b + 1) * tokens)
        pieces = [parts_of(held[2 * b + h]) for h in range(2)]
        for h in range(2):
            high_rows[h, here], low_rows[h, here] = pieces[h]
        sums = sum(product(pieces[h], (up_high[at[h], :], up_low[at[h], :]), 1) for h in range(2))
        back = sum(
            product(parts_of(held[8 + 2 * b + h]), (down_high[at[h], :], down_low[at[h], :]), 1)
            for h in range(2)
        )
        gate, lift = sums[:, :width], sums[:, width:]
        sigmoid = 1.0 / (1.0 + jnp.exp(-gate))
        back = back * sigmoid
        gate, lift = back * lift * (1.0 + gate * (1.0 - sigmoid)), back * gate
        grads = [x[:, u * unit : (u + 1) * unit] for u in range(units) for x in (gate, lift)]
        high_grads[here], low_grads[here] = parts_of(jnp.concatenate(grads, 1))
        if b % 2 == 1:
            pair = slice((b - 1) * tokens, (b + 1) * tokens)
            for h in range(2):
                term = product(
                    (high_rows[h, pair], low_rows[h, pair]),
                    (high_grads[pair], low_grads[pair]),
                    0,
                )
                total[h] = term if b == 1 else total[h] + term

    for h, place in ((0, side), (1, 1 - side)):
        for u in range(units):
            for bit in range(2):
                for ref, whose in ((keep_ref, bit), (send_ref, 1 - bit)):

                    @pl.when(core == whose)
                    def _():
                        for block in range(blocks):
                            start = (block * 2 + bit) * depth
                            ref[u, place * blocks + block] = total[
                                h, start : start + depth, u * 2 * unit : (u + 1) * 2 * unit
                            ]


def after(tree):
    leaves, shape = jax.tree.flatten(tree)
    return jax.tree.unflatten(shape, lax.optimization_barrier(leaves))


def make_local(n_dp, n_tensor):
    n_bits = n_dp.bit_length() - 1
    t_bits = n_tensor.bit_length() - 1

    def local(
        inputs,
        cotangent,
        gate_weight,
        up_weight,
        down_weight,
        gate_first,
        gate_second,
        up_first,
        up_second,
    ):
        bits = [Bit("dp", n_dp, place) for place in reversed(range(n_bits))]
        far, near, core = bits[0], bits[-2], bits[-1]
        middle = bits[1:-2]
        features = [Bit("tensor", n_tensor, place) for place in range(t_bits)]
        side = features[-1]
        depth, columns = gate_weight.shape
        part = columns // 4
        chunks = CHUNKS if part % (CHUNKS * 128) == 0 else 1
        width = part // chunks
        both = 2 * width
        sizes = [chunks // 2] + [1] * (chunks // 2) if chunks % 2 == 0 else [chunks]
        half = sizes[0] * width
        most = (chunks - chunks // 4) * width
        for bit in features[:-1]:
            inputs = bit.joined(inputs, bit.swap(inputs), 1)
            cotangent = bit.joined(cotangent, bit.swap(cotangent), 1)

        def columns_of(far_bit, near_bit):
            start = (far_bit * 2 + near_bit) * part
            return jnp.stack(
                [
                    lax.dynamic_slice_in_dim(weight, start, part, 1)
                    for weight in (gate_weight, up_weight, down_weight)
                ]
            )

        def over_middle(pair):
            moved = [pair]
            for bit in reversed(middle):
                moved = moved + [[bit.swap(x) for x in p] for p in moved]
            return moved

        def arranged(moved):
            blocks = [near.ordered(p[0], p[1], 0) for p in moved]
            for bit in middle:
                half_way = len(blocks) // 2
                blocks = [
                    bit.ordered(a, b, 0) for a, b in zip(blocks[:half_way], blocks[half_way:])
                ]
            return blocks[0].reshape((-1,) + blocks[0].shape[-3:])

        tokens = inputs.shape[0]

        pairs = [(i, i ^ (1 << (n_bits - 1)) ^ 2) for i in range(n_dp)]

        def diagonal(array):
            return lax.ppermute(array, "dp", pairs)

        oo = columns_of(far.mine, near.mine)
        ox = columns_of(far.mine, 1 - near.mine)
        xx = columns_of(1 - far.mine, 1 - near.mine)
        n_weight = 3 * depth * part // cotangent.shape[1]
        s = after(
            dict(
                in_far=far.swap(inputs),
                in_side=side.swap(inputs),
                cot_side=side.swap(cotangent),
                oo_near=near.swap(ox),
                in_near=near.swap(inputs),
                inputs=inputs,
                cotangent=cotangent,
                oo=oo,
                xo=columns_of(1 - far.mine, near.mine),
                by_near=jnp.concatenate([xx.reshape(n_weight, -1), cotangent], 0),
            )
        )

        by_near = near.swap(s["by_near"])
        s = after(
            dict(
                s,
                cot_far=far.swap(s["cotangent"]),
                in_far_side=side.swap(s["in_far"]),
                in_diag=side.swap(s["in_near"]),
                xo_near=by_near[:n_weight].reshape(3, depth, part),
                cot_near=by_near[n_weight:],
                kept=over_middle([s["oo"]]),
            )
        )

        by_far = far.swap(jnp.stack([s["xo"][..., :most], s["xo_near"][..., :most]]))
        by_near = near.swap(jnp.concatenate([s["in_far"], s["cot_far"]], 0))
        s = after(
            dict(
                s,
                come=by_far,
                send=jnp.stack([s["xo"][..., most:], s["xo_near"][..., most:]]),
                cot_diag=side.swap(s["cot_near"]),
                cot_far_side=side.swap(s["cot_far"]),
                in_far_near=by_near[:tokens],
                cot_far_near=by_near[tokens:],
                kept_near=over_middle([s["oo_near"]]),
            )
        )

        late = s["come"][..., half:]
        if most < part:
            late = (late, far.swap(s["send"]))
        kept = arranged([a + b for a, b in zip(s["kept"], s["kept_near"])])
        s = after(
            dict(
                s,
                late=late,
                in_far_diag=near.swap(s["in_far_side"]),
                cot_far_diag=side.swap(s["cot_far_near"]),
                kept=kept,
                kept_core=core.swap(kept),
                come=over_middle([s["come"][..., :half]]),
            )
        )
        come = arranged([[p[0][0], p[0][1]] for p in s["come"]])
        s = after(dict(s, come=come, come_core=core.swap(come)))
        tokens_of = [
            s[name]
            for name in (
                "inputs", "in_side", "in_near", "in_diag",
                "in_far", "in_far_side", "in_far_near", "in_far_diag",
                "cotangent", "cot_side", "cot_near", "cot_diag",
                "cot_far", "cot_far_side", "cot_far_near", "cot_far_diag",
            )
        ]
        mine = jnp.stack([side.mine, core.mine, far.mine]).astype(jnp.int32)

        def grads_of(ahead, units, kept_at, come_at, *arrays):
            held = units * width
            feature_rows = n_dp * depth
            out = jax.ShapeDtypeStruct((units, n_dp // 2, depth, both), jnp.float32)
            vmem = pl.BlockSpec(memory_space=pltpu.VMEM)
            any_space = pl.BlockSpec(memory_space=pl.ANY)
            all_tokens = 4 * tokens
            keep, send = pl.pallas_call(
                functools.partial(chunk_kernel, (kept_at, kept_at, come_at, come_at), held),
                out_shape=(out, out),
                in_specs=[pl.BlockSpec(memory_space=pltpu.SMEM)] + [any_space] * len(arrays),
                out_specs=(vmem, vmem),
                scratch_shapes=[
                    pltpu.VMEM((16,) + inputs.shape, jnp.float32),
                    pltpu.VMEM((4, n_dp // 4, 3, depth, held), jnp.float32),
                    pltpu.VMEM((feature_rows, 2 * held), jnp.bfloat16),
                    pltpu.VMEM((feature_rows, 2 * held), jnp.bfloat16),
                    pltpu.VMEM((feature_rows, held), jnp.bfloat16),
                    pltpu.VMEM((feature_rows, held), jnp.bfloat16),
                    pltpu.VMEM((2, all_tokens, feature_rows // 2), jnp.bfloat16),
                    pltpu.VMEM((2, all_tokens, feature_rows // 2), jnp.bfloat16),
                    pltpu.VMEM((all_tokens, 2 * held), jnp.bfloat16),
                    pltpu.VMEM((all_tokens, 2 * held), jnp.bfloat16),
                    pltpu.VMEM((2, feature_rows // 2, 2 * held), jnp.float32),
                    pltpu.SemaphoreType.DMA((20,)),
                ],
                compiler_params=pltpu.CompilerParams(vmem_limit_bytes=VMEM_LIMIT),
                cost_estimate=pl.CostEstimate(
                    flops=30 * all_tokens * feature_rows * held,
                    bytes_accessed=8 * all_tokens * feature_rows,
                    transcendentals=all_tokens * held,
                ),
            )(mine, *arrays)
            shape = [units] + [2] * (n_bits - 1) + [depth, both]
            send, ahead = after((send, ahead))
            return [keep.reshape(shape), core.swap(send).reshape(shape)], ahead

        kept, kept_core = s["kept"], s["kept_core"]
        arrived = (s["come"], s["come_core"])
        late = s["late"]
        calls = len(sizes)
        firsts = [sum(sizes[:call]) for call in range(calls)]
        stages = {}
        for step in range(calls + 2):
            new = {}
            for call in range(calls):
                if step == call + 2:
                    own, beside, beyond, across = stages[call]
                    own = near.ordered(own, near.swap(beside), 1)
                    beyond = near.ordered(far.swap(beyond), diagonal(across), 1)
                    new[call] = far.ordered(own, beyond, 2)
                if step == call + 1:
                    terms = stages[call]
                    for bit in middle:
                        keep, send = (
                            sum(part(x, 2) for x in terms) for part in (bit.own, bit.other)
                        )
                        terms = [keep, bit.swap(send)]
                    new[call] = [
                        sum(there(here(x, 1), 1) for x in terms)
                        for here in (far.own, far.other)
                        for there in (near.own, near.other)
                    ]
            if step < calls:
                fresh = None
                if step == 0 and calls > 1:
                    fresh = over_middle([jnp.concatenate(late, -1) if most < part else late])
                come_at = max(firsts[step] * width - half, 0)
                terms, (fresh, new) = grads_of(
                    (fresh, new), sizes[step], firsts[step] * width, come_at,
                    *tokens_of, kept, kept_core, *arrived,
                )
                new[step] = terms
                if step == 0 and calls > 1:
                    fresh = arranged([[p[0][0], p[0][1]] for p in fresh])
                    arrived = (fresh, core.swap(fresh))
            stages.update(new)
            if step < calls + 1:
                stages, kept, kept_core, tokens_of, arrived = after(
                    (stages, kept, kept_core, tokens_of, arrived)
                )

        pieces = []
        for call in range(calls):
            pieces += [stages[call][u] for u in range(sizes[call])]

        def assembled(which):
            return jnp.concatenate(
                [
                    pieces[chunk][n, f, :, which * width : (which + 1) * width]
                    for f in range(2)
                    for n in range(2)
                    for chunk in range(chunks)
                ],
                1,
            )

        gate_new, gate_first_new, gate_second_new = adam_update(
            gate_weight, gate_first, gate_second, assembled(0)
        )
        up_new, up_first_new, up_second_new = adam_update(
            up_weight, up_first, up_second, assembled(1)
        )
        return (gate_new, gate_first_new, gate_second_new, up_new, up_first_new, up_second_new)

    return local


def solution(mesh):
    spec = P("dp", "tensor")
    local = make_local(mesh.shape["dp"], mesh.shape["tensor"])
    return jax.shard_map(
        local, mesh=mesh, in_specs=(spec,) * 9, out_specs=(spec,) * 6, check_vma=False
    )
```
